256 devices in a mesh: row: 16 (over x_hi, y, core), col: 16 (over z, x_lo).
Axes of the slice: x: 4 (x_hi: 2, x_lo: 2; x = x_hi * 2 + x_lo), y: 4, z: 8, core: 2. Of those that a mesh axis runs over, the one named last changes fastest.
Arguments:
- coords: float32 [2, 131072], P(None, 'row'), may hold values from 0 to 1
- order: int32 [131072], replicated, may hold values from 0 to 131071, as said below
- panel_index: int32 [1], replicated, may hold values from 0 to 253
- trailing: float32 [16, 16, 1024, 512], P(None, 'row', 'col'), may hold values from -6 to 6
Outputs:
- panel_factor: float32 [16, 16, 512, 512], P(None, 'row', 'col')
- new_trailing: float32 [16, 16, 1024, 512], P(None, 'row', 'col')
The draws below stay inside these ranges and needn't reach their ends.
Inputs may be any that keep to these rules, and one draw needn't show every extreme that they name: order is a permutation of the matrix indices that maps index m to a location of the same owner range: m // 8192 == order[m] // 8192.
All inputs are finite; a program needn't handle non-finite values.
Results may differ from the reference program's by a relative error of at most 0.0003.
Values sent between devices are 32-bit elements; how exact they have to be, the bound alone decides.
No kernel may reach another device: no remote copies, remote signals or barrier semaphores. Data moves between devices by JAX's collectives and lax.ppermute only.
A program may use at most 128 MiB of HBM per device.

```python
import math
import jax
import jax.numpy as jnp
from jax import lax

B = 512
LB = 16
NBLK = 256
N = 131072
N_ROW = 16


def draw_order(key, part):
    key = jax.random.fold_in(key, 7)
    owned = LB * B
    keys = jax.random.split(key, N_ROW)
    perms = jax.vmap(lambda one_key: jax.random.permutation(one_key, owned))(keys)
    offsets = (jnp.arange(N_ROW, dtype=jnp.int32) * owned)[:, None]
    return (perms.astype(jnp.int32) + offsets).reshape(-1)


def block_scale(key, shape, cuts, low, high):
    def one(dim, parts):
        draws = jax.random.uniform(jax.random.fold_in(jax.random.fold_in(key, 6), dim), (parts,), jnp.float32, low / len(cuts), high / len(cuts))
        return jnp.repeat(jnp.exp(draws), shape[dim] // parts).reshape((-1,) + (1,) * (len(shape) - dim - 1))

    factor_of = one(*cuts[0])
    for cut in cuts[1:]:
        factor_of = factor_of * one(*cut)
    return factor_of


def scatter_about(rng, dims, deviation, bound, shards=(), kind=jnp.bfloat16):
    level = block_scale(rng, dims, shards, -0.22, 0.18) if shards else 1.0
    values = jax.random.normal(rng, dims, jnp.float32) * deviation * level
    return jnp.minimum(jnp.maximum(values, -bound), bound).astype(kind)


def setup_inputs(seed: int = 0) -> dict:
    key_list = jax.random.split(jax.random.key(seed), 5)
    return {
        "coords": jnp.clip(1.0 * jax.random.uniform(key_list[0], (2, N), jnp.float32) ** block_scale(key_list[0], (2, N), ((1, 16),), -0.2, 0.2), 0.0, 1.0),
        "order": draw_order(jax.random.fold_in(key_list[4], 71), 0),
        "panel_index": jax.random.randint(key_list[2], (1,), 0, NBLK - 2).astype(jnp.int32),
        "trailing": scatter_about(key_list[3], (LB, N_ROW, 2 * B, B), 1.0, 6.0, ((1, 16), (2, 16)), jnp.float32),
    }


ROOT_THREE = math.sqrt(3.0)
LENGTH = 0.05
NUGGET = 1.0

def matern(row_x, row_y, col_x, col_y):
    diff_x = row_x[..., :, None] - col_x
    diff_y = row_y[..., :, None] - col_y
    scaled = ROOT_THREE / LENGTH * jnp.sqrt(diff_x * diff_x + diff_y * diff_y)
    return (1.0 + scaled) * jnp.exp(-scaled)

def right_solve(factor, rows):
    return lax.linalg.triangular_solve(factor, rows, left_side=False, lower=True, transpose_a=True)

def reference(coords, order, panel_index, trailing):
    located = jnp.take(coords, order, axis=1)
    start = panel_index[0] * B
    pivot = lax.dynamic_slice_in_dim(located, start, 3 * B, 1)
    pivot_x = pivot[0, :B]
    pivot_y = pivot[1, :B]
    pivot_ids = start + jnp.arange(B, dtype=jnp.int32)
    diag = matern(pivot_x, pivot_y, pivot_x, pivot_y) + NUGGET * jnp.eye(B, dtype=jnp.float32)
    factor = jnp.linalg.cholesky(diag)
    far = matern(pivot[0, B:], pivot[1, B:], pivot_x, pivot_y)
    far_factor = right_solve(factor, far)
    blocks_xy = located.reshape(2, NBLK, B)
    block_k = panel_index[0]

    def one_block(block):
        row_ids = block * B + jnp.arange(B, dtype=jnp.int32)
        nugget = NUGGET * (row_ids[:, None] == pivot_ids[None, :]).astype(jnp.float32)
        cov = matern(blocks_xy[0, block], blocks_xy[1, block], pivot_x, pivot_y) + nugget
        solved = right_solve(factor, cov)
        solved = jnp.where(block >= block_k, solved, jnp.zeros_like(solved))
        update = jnp.dot(far_factor, solved.T, precision=lax.Precision.HIGHEST)
        return (solved, jnp.where(block > block_k, update, jnp.zeros_like(update)))
    panel, updates = lax.map(one_block, jnp.arange(NBLK, dtype=jnp.int32))
    panel_factor = panel.reshape(LB, N_ROW, B, B)
    new_trailing = trailing - updates.reshape(LB, N_ROW, 2 * B, B)
    return (panel_factor, new_trailing)
```

```python
import functools
import math

import jax
import jax.numpy as jnp
from jax import lax
from jax.experimental import pallas as pl
from jax.experimental.pallas import tpu as pltpu
from jax.sharding import PartitionSpec as P

B = 512
LB = 16
OWNED = LB * B
LANES = 128
ROOT_THREE = math.sqrt(3.0)
LENGTH = 0.05
NUGGET = 1.0
F32 = jnp.float32
BF16 = jnp.bfloat16


def matern(row_x, row_y, col_x, col_y):
    diff_x = row_x - col_x
    diff_y = row_y - col_y
    square = diff_x * diff_x + diff_y * diff_y
    scaled = (ROOT_THREE / LENGTH) * square * lax.rsqrt(jnp.maximum(square, 1e-30))
    return (1.0 + scaled) * jnp.exp(-scaled)


def split2(value):
    high = value.astype(BF16)
    return high, (value - high.astype(F32)).astype(BF16)


def dot3(a, b, dims):
    a_high, a_low = split2(a)
    b_high, b_low = split2(b)
    product = functools.partial(
        lax.dot_general, dimension_numbers=(dims, ((), ())), preferred_element_type=F32
    )
    return product(a_high, b_high) + (product(a_high, b_low) + product(a_low, b_high))


def locate_kernel(panel_ref, order_ref, coords_ref, out_ref, index_ref, table_ref, found_ref, sem):
    here = lax.axis_index("row")
    rows = OWNED // LANES
    copy = pltpu.make_async_copy(order_ref.at[pl.ds(here * rows, rows), :], index_ref, sem)
    copy.start()
    for high in range(rows):
        at = slice(high * LANES, (high + 1) * LANES)
        table_ref[high : high + 1, :LANES] = coords_ref[0:1, at]
        table_ref[high : high + 1, LANES:] = coords_ref[1:2, at]
    table = table_ref[...]
    first = table.astype(BF16)
    rest = table - first.astype(F32)
    second = rest.astype(BF16)
    third = (rest - second.astype(F32)).astype(BF16)
    pieces = jnp.concatenate([first, second, third], axis=0)
    copy.wait()
    high_iota = lax.broadcasted_iota(jnp.int32, (rows, B), 0)
    low_iota = lax.broadcasted_iota(jnp.int32, (LANES, B), 0)
    for block in range(LB):
        per = B // LANES
        index = jnp.concatenate(
            [index_ref[block * per + t : block * per + t + 1, :] for t in range(per)], axis=1
        )
        index = index - here * OWNED
        high = (high_iota == (index >> 7)).astype(F32).astype(BF16)
        spread = lax.dot_general(
            pieces,
            jnp.concatenate([high, high, high], axis=0),
            (((0,), (0,)), ((), ())),
            preferred_element_type=F32,
        )
        chosen = low_iota == (index & (LANES - 1))
        x = jnp.sum(jnp.where(chosen, spread[:LANES], 0.0), axis=0, keepdims=True)
        y = jnp.sum(jnp.where(chosen, spread[LANES:], 0.0), axis=0, keepdims=True)
        found_ref[block, 0:1, :] = x
        found_ref[block, 1:2, :] = y
        out_ref[block, 0:1, :] = x
        out_ref[block, 1:2, :] = y
    for ahead in range(3):
        local = jnp.clip(panel_ref[0] + ahead - here * LB, 0, LB - 1)
        pivot = found_ref[local]
        for block in range(LB):
            out_ref[block, 2 + 2 * ahead : 4 + 2 * ahead, :] = pivot


def locate(panel_index, order, coords):
    return pl.pallas_call(
        locate_kernel,
        out_shape=jax.ShapeDtypeStruct((LB, 8, B), F32),
        in_specs=[
            pl.BlockSpec(memory_space=pltpu.SMEM),
            pl.BlockSpec(memory_space=pl.ANY),
            pl.BlockSpec(memory_space=pltpu.VMEM),
        ],
        out_specs=pl.BlockSpec(memory_space=pltpu.VMEM),
        scratch_shapes=[
            pltpu.VMEM((OWNED // LANES, LANES), jnp.int32),
            pltpu.VMEM((OWNED // LANES, 2 * LANES), F32),
            pltpu.VMEM((LB, 2, B), F32),
            pltpu.SemaphoreType.DMA,
        ],
        name="locate",
    )(panel_index, order.reshape(-1, LANES), coords)


def update_kernel(
    panel_ref, own_ref, far_ref, pivot_ref, got_ref, inverse_ref, trailing_ref,
    panel_out, trailing_out, weight_ref, solved_ref, wide_ref,
):
    step = pl.program_id(0)
    here_row = lax.axis_index("row")
    here_col = lax.axis_index("col")
    block_k = panel_ref[0]
    share = solved_ref.shape[0] // LB
    span = weight_ref.shape[0]
    block = step * LB + here_row

    @pl.when(step == 0)
    def _():
        pivot = pivot_ref[...]
        pivot_x = pivot[0:1, :]
        pivot_y = pivot[1:2, :]
        columns = pivot.T
        wide_ref[0] = jnp.broadcast_to(columns[:, 0:1], (B, LANES))
        wide_ref[1] = jnp.broadcast_to(columns[:, 1:2], (B, LANES))
        inverse = inverse_ref[...]
        far = far_ref[...].T
        far_cov = matern(far[:, 0:1], far[:, 1:2], pivot_x, pivot_y)
        far_factor = dot3(far_cov, inverse, ((1,), (1,)))
        weight_ref[...] = dot3(far_factor, inverse, ((1,), (0,)))
        own = own_ref[...].T
        cov = matern(own[:, 0:1], own[:, 1:2], pivot_x, pivot_y)
        position = lax.broadcasted_iota(jnp.int32, (LB * share, B), 0)
        column = lax.broadcasted_iota(jnp.int32, (LB * share, B), 1)
        blocks = (position // share) * LB + here_row
        within = here_col * share + position % share
        cov = cov + jnp.where((blocks == block_k) & (within == column), NUGGET, 0.0)
        solved = dot3(cov, inverse, ((1,), (1,)))
        solved_ref[...] = jnp.where(blocks >= block_k, solved, 0.0)

    panel_out[0, 0] = solved_ref[pl.ds(step * share, share), :]

    @pl.when(block > block_k)
    def _():
        weight_high, weight_low = split2(weight_ref[...])
        for part in range(B // LANES):
            at = slice(part * LANES, (part + 1) * LANES)
            cov = matern(wide_ref[0], wide_ref[1], got_ref[0, 0:1, at], got_ref[0, 1:2, at])
            cov_high, cov_low = split2(cov)
            update = jnp.dot(weight_high, cov_high, preferred_element_type=F32) + (
                jnp.dot(weight_high, cov_low, preferred_element_type=F32)
                + jnp.dot(weight_low, cov_high, preferred_element_type=F32)
            )
            trailing_out[0, 0, :, at] = trailing_ref[0, 0, :, at] - update

    @pl.when(block <= block_k)
    def _():
        trailing_out[...] = trailing_ref[...]


def update(panel_index, own, far, pivot, got, inverse, trailing, share):
    span = trailing.shape[2]
    whole = lambda *shape: pl.BlockSpec(shape, lambda i: (0,) * len(shape))
    return pl.pallas_call(
        update_kernel,
        grid=(LB,),
        out_shape=(
            jax.ShapeDtypeStruct((LB, 1, share, B), F32),
            jax.ShapeDtypeStruct(trailing.shape, F32),
        ),
        in_specs=[
            pl.BlockSpec(memory_space=pltpu.SMEM),
            whole(8, LB * share),
            whole(8, span),
            whole(8, B),
            pl.BlockSpec((1, 8, B), lambda i: (i, 0, 0)),
            whole(B, B),
            pl.BlockSpec((1, 1, span, B), lambda i: (i, 0, 0, 0)),
        ],
        out_specs=(
            pl.BlockSpec((1, 1, share, B), lambda i: (i, 0, 0, 0)),
            pl.BlockSpec((1, 1, span, B), lambda i: (i, 0, 0, 0)),
        ),
        scratch_shapes=[
            pltpu.VMEM((span, B), F32),
            pltpu.VMEM((LB * share, B), F32),
            pltpu.VMEM((2, B, LANES), F32),
        ],
        compiler_params=pltpu.CompilerParams(vmem_limit_bytes=40 * 1024 * 1024),
        name="update",
    )(panel_index, own, far, pivot, got, inverse, trailing)


def on_device(coords, order, panel_index, trailing):
    columns = lax.axis_size("col")
    here_col = lax.axis_index("col")
    span = trailing.shape[2]
    share = B // columns
    block_k = panel_index[0]
    got = lax.all_to_all(locate(panel_index, order, coords), "row", 0, 0, tiled=True)

    def pivot_block(ahead):
        block = block_k + ahead
        return lax.dynamic_index_in_dim(got, block // LB, 0, keepdims=False)[
            2 + 2 * ahead : 4 + 2 * ahead
        ]

    pad = lambda pair: jnp.pad(pair, ((0, 6), (0, 0)))
    pivot = pivot_block(0)
    far = jnp.concatenate([pivot_block(1), pivot_block(2)], axis=1)
    far = lax.dynamic_slice_in_dim(far, here_col * span, span, 1)
    own = lax.dynamic_slice_in_dim(got[:, 0:2], here_col * share, share, 2)
    own = own.transpose(1, 0, 2).reshape(2, LB * share)
    diag = matern(pivot[0][:, None], pivot[1][:, None], pivot[0], pivot[1])
    diag = diag + NUGGET * jnp.eye(B, dtype=F32)
    factor = jnp.linalg.cholesky(diag)
    inverse = lax.linalg.triangular_solve(
        factor, jnp.eye(B, dtype=F32), left_side=True, lower=True
    )
    return update(panel_index, pad(own), pad(far), pad(pivot), got, inverse, trailing, share)


def solution(mesh):
    placed = (P(None, "row"), P(), P(), P(None, "row", "col", None))
    return jax.shard_map(
        on_device,
        mesh=mesh,
        in_specs=placed,
        out_specs=(P(None, "row", "col", None), P(None, "row", "col", None)),
        check_vma=False,
    )
```

```python
import functools
import math

import jax
import jax.numpy as jnp
from jax import lax
from jax.experimental import pallas as pl
from jax.experimental.pallas import tpu as pltpu
from jax.sharding import PartitionSpec as P

B = 512
LB = 16
OWNED = LB * B
LANES = 128
ROOT_THREE = math.sqrt(3.0)
LENGTH = 0.05
NUGGET = 1.0
F32 = jnp.float32
BF16 = jnp.bfloat16


def matern(row_x, row_y, col_x, col_y):
    diff_x = row_x - col_x
    diff_y = row_y - col_y
    square = diff_x * diff_x + diff_y * diff_y
    scaled = (ROOT_THREE / LENGTH) * square * lax.rsqrt(jnp.maximum(square, 1e-30))
    return (1.0 + scaled) * jnp.exp(-scaled)


def split2(value):
    high = value.astype(BF16)
    return high, (value - high.astype(F32)).astype(BF16)


def dot3(a, b, dims):
    a_high, a_low = split2(a)
    b_high, b_low = split2(b)
    product = functools.partial(
        lax.dot_general, dimension_numbers=(dims, ((), ())), preferred_element_type=F32
    )
    return product(a_high, b_high) + (product(a_high, b_low) + product(a_low, b_high))


def locate_kernel(panel_ref, order_ref, coords_ref, out_ref, index_ref, table_ref, found_ref, sem):
    here = lax.axis_index("row")
    rows = OWNED // LANES
    copy = pltpu.make_async_copy(order_ref.at[pl.ds(here * rows, rows), :], index_ref, sem)
    copy.start()
    for high in range(rows):
        at = slice(high * LANES, (high + 1) * LANES)
        table_ref[high : high + 1, :LANES] = coords_ref[0:1, at]
        table_ref[high : high + 1, LANES:] = coords_ref[1:2, at]
    table = table_ref[...]
    first = table.astype(BF16)
    rest = table - first.astype(F32)
    second = rest.astype(BF16)
    third = (rest - second.astype(F32)).astype(BF16)
    pieces = jnp.concatenate([first, second, third], axis=0)
    copy.wait()
    high_iota = lax.broadcasted_iota(jnp.int32, (rows, B), 0)
    low_iota = lax.broadcasted_iota(jnp.int32, (LANES, B), 0)
    for block in range(LB):
        per = B // LANES
        index = jnp.concatenate(
            [index_ref[block * per + t : block * per + t + 1, :] for t in range(per)], axis=1
        )
        index = index - here * OWNED
        high = (high_iota == (index >> 7)).astype(F32).astype(BF16)
        spread = lax.dot_general(
            pieces,
            jnp.concatenate([high, high, high], axis=0),
            (((0,), (0,)), ((), ())),
            preferred_element_type=F32,
        )
        chosen = low_iota == (index & (LANES - 1))
        x = jnp.sum(jnp.where(chosen, spread[:LANES], 0.0), axis=0, keepdims=True)
        y = jnp.sum(jnp.where(chosen, spread[LANES:], 0.0), axis=0, keepdims=True)
        found_ref[block, 0:1, :] = x
        found_ref[block, 1:2, :] = y
        out_ref[block, 0:1, :] = x
        out_ref[block, 1:2, :] = y
    for ahead in range(3):
        local = jnp.clip(panel_ref[0] + ahead - here * LB, 0, LB - 1)
        pivot = found_ref[local]
        for block in range(LB):
            out_ref[block, 2 + 2 * ahead : 4 + 2 * ahead, :] = pivot


def locate(panel_index, order, coords):
    return pl.pallas_call(
        locate_kernel,
        out_shape=jax.ShapeDtypeStruct((LB, 8, B), F32),
        in_specs=[
            pl.BlockSpec(memory_space=pltpu.SMEM),
            pl.BlockSpec(memory_space=pl.ANY),
            pl.BlockSpec(memory_space=pltpu.VMEM),
        ],
        out_specs=pl.BlockSpec(memory_space=pltpu.VMEM),
        scratch_shapes=[
            pltpu.VMEM((OWNED // LANES, LANES), jnp.int32),
            pltpu.VMEM((OWNED // LANES, 2 * LANES), F32),
            pltpu.VMEM((LB, 2, B), F32),
            pltpu.SemaphoreType.DMA,
        ],
        name="locate",
    )(panel_index, order.reshape(-1, LANES), coords)


TILE = 8
CORE = 64


def column_of(value, at):
    return jnp.broadcast_to(value[:, at : at + 1], (TILE, LANES))


def row_of(value, at):
    return jnp.broadcast_to(value[at : at + 1, :], (TILE, LANES))


def inverse_factor(rows):
    rows = list(rows)
    count = len(rows)
    sub = lax.broadcasted_iota(jnp.int32, (TILE, LANES), 0)
    lane = lax.broadcasted_iota(jnp.int32, (TILE, LANES), 1)
    others = [(sub != i).astype(F32) for i in range(TILE)]
    below = [(sub > i).astype(F32) for i in range(TILE)]

    def columns(row, panel):
        return [column_of(rows[row], TILE * panel + c) for c in range(TILE)]

    ahead = columns(0, 0)
    for j in range(count):
        last = j == count - 1
        inside = (lane >= TILE * j) & (lane < TILE * (j + 1))
        left = [columns(i, j) for i in range(j + 1, count)]
        here = list(ahead)
        if not last:
            next_left = list(left[0])
            ahead = columns(j + 1, j + 1)
        lower = jnp.where(inside, (lane - TILE * j == sub).astype(F32), rows[j])
        both = lower
        scale = jnp.ones((TILE, LANES), F32)
        for i in range(TILE):
            inverse_pivot = 1.0 / row_of(here[i], i)
            by_others = here[i] * (inverse_pivot * others[i])
            by_below = here[i] * (inverse_pivot * below[i])
            if not last:
                by_next = next_left[i] * inverse_pivot
            for c in range(i + 1, TILE):
                pivot_row = row_of(here[c], i)
                here[c] = here[c] - by_others * pivot_row
                if not last:
                    next_left[c] = next_left[c] - by_next * pivot_row
            if not last:
                for c in range(TILE):
                    ahead[c] = ahead[c] - by_next * row_of(next_left[i], c)
            lower = lower - by_below * row_of(lower, i)
            both = both - by_others * row_of(both, i)
            scale = jnp.where(sub == i, inverse_pivot, scale)
        rows[j] = lower * lax.rsqrt(1.0 / scale)
        if last:
            break
        both = both * scale
        spread = [row_of(both, c) for c in range(TILE)]
        for i in range(j + 1, count):
            terms = [left[i - j - 1][c] * spread[c] for c in range(TILE)]
            while len(terms) > 1:
                terms = [terms[t] + terms[t + 1] for t in range(0, len(terms), 2)]
            rows[i] = jnp.where(inside, 0.0, rows[i]) - terms[0]
    return rows


def split3(value):
    first = value.astype(BF16)
    rest = value - first.astype(F32)
    second = rest.astype(BF16)
    return first, second, (rest - second.astype(F32)).astype(BF16)


def dot6(a, b, dims):
    a1, a2, a3 = split3(a)
    b1, b2, b3 = split3(b)
    left, right = dims
    return lax.dot_general(
        jnp.concatenate([a1, a2, a1, a2, a1, a3], axis=left),
        jnp.concatenate([b1, b1, b2, b2, b3, b1], axis=right),
        (((left,), (right,)), ((), ())),
        preferred_element_type=F32,
    )


def factor_in_place(matrix):
    order = matrix.shape[0]
    for start in range(0, order, CORE):
        base = start // LANES * LANES
        half = start - base
        block = matrix[start : start + CORE, base : base + LANES]
        if half:
            block = pltpu.roll(block, LANES - half, 1)
        core = jnp.concatenate(
            inverse_factor([block[t : t + TILE] for t in range(0, CORE, TILE)]), axis=0
        )[:, :CORE]
        sub = lax.broadcasted_iota(jnp.int32, (CORE, CORE), 0)
        lane = lax.broadcasted_iota(jnp.int32, (CORE, CORE), 1)
        core = jnp.where(sub >= lane, core, 0.0)
        zero = jnp.zeros((CORE, CORE), F32)
        placed = jnp.concatenate([zero, core] if half else [core, zero], axis=1)
        rest = order - start - CORE
        if rest:
            below = matrix[start + CORE :, base : base + LANES]
            factor = dot6(below, placed, (1, 1))
        solved = dot6(core, matrix[start : start + CORE, :], (1, 0))
        lane = lax.broadcasted_iota(jnp.int32, (CORE, LANES), 1)
        inside = (lane >= half) & (lane < half + CORE)
        parts = [solved[:, at : at + LANES] for at in range(0, order, LANES)]
        parts[base // LANES] = jnp.where(inside, placed, parts[base // LANES])
        solved = jnp.concatenate(parts, axis=1)
        matrix[start : start + CORE, :] = solved
        if rest:
            lane = lax.broadcasted_iota(jnp.int32, (rest, LANES), 1)
            inside = (lane >= half) & (lane < half + CORE)
            matrix[start + CORE :, base : base + LANES] = jnp.where(inside, 0.0, below)
            matrix[start + CORE :, :] = matrix[start + CORE :, :] - dot6(factor, solved, (1, 0))


def update_kernel(
    panel_ref, got_ref, trailing_ref,
    panel_out, trailing_out, weight_ref, solved_ref, wide_ref, matrix_ref, turned_ref,
):
    step = pl.program_id(0)
    here_row = lax.axis_index("row")
    here_col = lax.axis_index("col")
    block_k = panel_ref[0]
    share = solved_ref.shape[0] // LB
    span = weight_ref.shape[0]
    block = step * LB + here_row

    @pl.when(step == 0)
    def _():
        pivot = got_ref[block_k // LB]
        pivot_x = pivot[2:3, :]
        pivot_y = pivot[3:4, :]
        turned = pivot.T
        wide_ref[0] = jnp.broadcast_to(turned[:, 2:3], (B, LANES))
        wide_ref[1] = jnp.broadcast_to(turned[:, 3:4], (B, LANES))
        for part in range(B // LANES):
            at = slice(part * LANES, (part + 1) * LANES)
            cov = matern(wide_ref[0], wide_ref[1], pivot_x[:, at], pivot_y[:, at])
            row = lax.broadcasted_iota(jnp.int32, (B, LANES), 0)
            lane = lax.broadcasted_iota(jnp.int32, (B, LANES), 1) + part * LANES
            matrix_ref[:, at] = cov + jnp.where(row == lane, NUGGET, 0.0)
        factor_in_place(matrix_ref)
        row = lax.broadcasted_iota(jnp.int32, (B, B), 0)
        column = lax.broadcasted_iota(jnp.int32, (B, B), 1)
        inverse = jnp.where(row >= column, matrix_ref[...], 0.0)

        spans = B // span
        ahead = 1 + here_col // spans
        turned_ref[:, :TILE] = got_ref[(block_k + ahead) // LB].T
        far = turned_ref[pl.ds(here_col % spans * span, span), :TILE]
        far_x = jnp.where(ahead == 1, far[:, 4:5], far[:, 6:7])
        far_y = jnp.where(ahead == 1, far[:, 5:6], far[:, 7:8])
        far_factor = dot3(matern(far_x, far_y, pivot_x, pivot_y), inverse, ((1,), (1,)))
        weight_ref[...] = dot3(far_factor, inverse, ((1,), (0,)))

        turned_ref[...] = got_ref[...].reshape(LB * TILE, B).T
        own = turned_ref[pl.ds(here_col * share, share), :]
        cov = jnp.concatenate(
            [
                matern(own[:, t : t + 1], own[:, t + 1 : t + 2], pivot_x, pivot_y)
                for t in range(0, LB * TILE, TILE)
            ],
            axis=0,
        )
        position = lax.broadcasted_iota(jnp.int32, (LB * share, B), 0)
        column = lax.broadcasted_iota(jnp.int32, (LB * share, B), 1)
        blocks = (position // share) * LB + here_row
        within = here_col * share + position % share
        cov = cov + jnp.where((blocks == block_k) & (within == column), NUGGET, 0.0)
        solved = dot3(cov, inverse, ((1,), (1,)))
        solved_ref[...] = jnp.where(blocks >= block_k, solved, 0.0)

    panel_out[0, 0] = solved_ref[pl.ds(step * share, share), :]

    @pl.when(block > block_k)
    def _():
        weight_high, weight_low = split2(weight_ref[...])
        for part in range(B // LANES):
            at = slice(part * LANES, (part + 1) * LANES)
            x = got_ref[step, 0:1, at]
            y = got_ref[step, 1:2, at]
            cov_high, cov_low = split2(matern(wide_ref[0], wide_ref[1], x, y))
            product = functools.partial(jnp.dot, preferred_element_type=F32)
            update = product(weight_high, cov_high) + (
                product(weight_high, cov_low) + product(weight_low, cov_high)
            )
            trailing_out[0, 0, :, at] = trailing_ref[0, 0, :, at] - update

    @pl.when(block <= block_k)
    def _():
        trailing_out[...] = trailing_ref[...]


def update(panel_index, got, trailing, share):
    span = trailing.shape[2]
    return pl.pallas_call(
        update_kernel,
        grid=(LB,),
        out_shape=(
            jax.ShapeDtypeStruct((LB, 1, share, B), F32),
            jax.ShapeDtypeStruct(trailing.shape, F32),
        ),
        in_specs=[
            pl.BlockSpec(memory_space=pltpu.SMEM),
            pl.BlockSpec(got.shape, lambda i: (0, 0, 0)),
            pl.BlockSpec((1, 1, span, B), lambda i: (i, 0, 0, 0)),
        ],
        out_specs=(
            pl.BlockSpec((1, 1, share, B), lambda i: (i, 0, 0, 0)),
            pl.BlockSpec((1, 1, span, B), lambda i: (i, 0, 0, 0)),
        ),
        scratch_shapes=[
            pltpu.VMEM((span, B), F32),
            pltpu.VMEM((LB * share, B), F32),
            pltpu.VMEM((2, B, LANES), F32),
            pltpu.VMEM((B, B), F32),
            pltpu.VMEM((B, LANES), F32),
        ],
        compiler_params=pltpu.CompilerParams(vmem_limit_bytes=48 * 1024 * 1024),
        name="update",
    )(panel_index, got, trailing)


def on_device(coords, order, panel_index, trailing):
    share = B // lax.axis_size("col")
    got = lax.all_to_all(locate(panel_index, order, coords), "row", 0, 0, tiled=True)
    return update(panel_index, got, trailing, share)


def solution(mesh):
    placed = (P(None, "row"), P(), P(), P(None, "row", "col", None))
    return jax.shard_map(
        on_device,
        mesh=mesh,
        in_specs=placed,
        out_specs=(P(None, "row", "col", None), P(None, "row", "col", None)),
        check_vma=False,
    )
```

```python
import functools
import math

import jax
import jax.numpy as jnp
from jax import lax
from jax.experimental import pallas as pl
from jax.experimental.pallas import tpu as pltpu
from jax.sharding import PartitionSpec as P

B = 512
LB = 16
OWNED = LB * B
LANES = 128
PER = B // LANES
SCALE = math.sqrt(3.0) / 0.05
ROOT_THREE = math.sqrt(3.0)
LENGTH = 0.05
NUGGET = 1.0
F32 = jnp.float32
BF16 = jnp.bfloat16


def matern(row_x, row_y, col_x, col_y):
    diff_x = row_x - col_x
    diff_y = row_y - col_y
    square = diff_x * diff_x + diff_y * diff_y
    scaled = (ROOT_THREE / LENGTH) * square * lax.rsqrt(jnp.maximum(square, 1e-30))
    return (1.0 + scaled) * jnp.exp(-scaled)


def split2(value):
    high = value.astype(BF16)
    return high, (value - high.astype(F32)).astype(BF16)


def split3(value):
    first = value.astype(BF16)
    rest = value - first.astype(F32)
    second = rest.astype(BF16)
    return first, second, (rest - second.astype(F32)).astype(BF16)


def locate_kernel(panel_ref, order_ref, coords_ref, out_ref, index_ref, pair_ref, table_ref, found_ref, sems):
    here = lax.axis_index("row")
    here_col = lax.axis_index("col")
    rows = OWNED // LANES
    order_copy = pltpu.make_async_copy(
        order_ref.at[pl.ds(here * rows, rows), :], index_ref, sems.at[0]
    )
    coords_copy = pltpu.make_async_copy(coords_ref, pair_ref, sems.at[1])
    order_copy.start()
    coords_copy.start()
    coords_copy.wait()
    for high in range(rows):
        at = slice(high * LANES, (high + 1) * LANES)
        table_ref[high : high + 1, :LANES] = pair_ref[0:1, at]
        table_ref[high : high + 1, LANES:] = pair_ref[1:2, at]
    pieces = jnp.concatenate(split3(table_ref[...]), axis=0)
    order_copy.wait()
    high_iota = lax.broadcasted_iota(jnp.int32, (rows, B), 0)
    low_iota = lax.broadcasted_iota(jnp.int32, (LANES, B), 0)
    for block in range(LB):
        index = jnp.concatenate(
            [index_ref[block * PER + t : block * PER + t + 1, :] for t in range(PER)], axis=1
        )
        index = index - here * OWNED
        high = (high_iota == (index >> 7)).astype(F32).astype(BF16)
        spread = lax.dot_general(
            pieces,
            jnp.concatenate([high, high, high], axis=0),
            (((0,), (0,)), ((), ())),
            preferred_element_type=F32,
        )
        chosen = low_iota == (index & (LANES - 1))
        for axis in range(2):
            part = spread[axis * LANES : (axis + 1) * LANES]
            value = jnp.sum(jnp.where(chosen, part, 0.0), axis=0, keepdims=True)
            for t in range(PER):
                found_ref[block, axis * PER + t : axis * PER + t + 1, :] = value[
                    :, t * LANES : (t + 1) * LANES
                ]
    pivot = found_ref[jnp.clip(panel_ref[0] - here * LB, 0, LB - 1)]
    ahead = 1 + here_col // (2 * PER)
    local = jnp.clip(panel_ref[0] + ahead - here * LB, 0, LB - 1)
    line = here_col // 2 % PER
    far_x = found_ref[local, pl.ds(line, 1), :]
    far_y = found_ref[local, pl.ds(PER + line, 1), :]
    low = lax.broadcasted_iota(jnp.int32, (1, LANES), 1) < LANES // 2
    even = jnp.where(low, far_x, pltpu.roll(far_y, LANES // 2, 1))
    odd = jnp.where(low, pltpu.roll(far_x, LANES // 2, 1), far_y)
    far = jnp.broadcast_to(jnp.where(here_col % 2 == 0, even, odd), (2 * PER, LANES))
    for block in range(LB):
        out_ref[block, 0 : 2 * PER, :] = found_ref[block]
        out_ref[block, 2 * PER : 4 * PER, :] = pivot
        out_ref[block, 4 * PER : 6 * PER, :] = far


def locate(panel_index, order, coords):
    return pl.pallas_call(
        locate_kernel,
        out_shape=jax.ShapeDtypeStruct((LB, 6 * PER, LANES), F32),
        in_specs=[
            pl.BlockSpec(memory_space=pltpu.SMEM),
            pl.BlockSpec(memory_space=pl.ANY),
            pl.BlockSpec(memory_space=pl.ANY),
        ],
        out_specs=pl.BlockSpec(memory_space=pltpu.VMEM),
        scratch_shapes=[
            pltpu.VMEM((OWNED // LANES, LANES), jnp.int32),
            pltpu.VMEM(coords.shape, F32),
            pltpu.VMEM((OWNED // LANES, 2 * LANES), F32),
            pltpu.VMEM((LB, 2 * PER, LANES), F32),
            pltpu.SemaphoreType.DMA((2,)),
        ],
        name="locate",
    )(panel_index, order.reshape(-1, LANES), coords)


TILE = 8
CORE = 64
ROWS = 128
COLS = 256


def column_of(value, at):
    return jnp.broadcast_to(value[:, at : at + 1], (TILE, LANES))


def row_of(value, at):
    return jnp.broadcast_to(value[at : at + 1, :], (TILE, LANES))


def inverse_factor(rows, offset):
    rows = list(rows)
    count = len(rows)
    sub = lax.broadcasted_iota(jnp.int32, (TILE, LANES), 0)
    lane = lax.broadcasted_iota(jnp.int32, (TILE, LANES), 1)
    others = [(sub != i).astype(F32) for i in range(TILE)]
    below = [(sub > i).astype(F32) for i in range(TILE)]

    def columns(row, panel):
        return [column_of(rows[row], offset + TILE * panel + c) for c in range(TILE)]

    here, left1, ahead11 = columns(0, 0), columns(1, 0), columns(1, 1)
    for j in range(count):
        first = offset + TILE * j
        one, two = j + 1 < count, j + 2 < count
        left = []
        if one:
            left.append(list(left1))
        if two:
            left2, ahead21, ahead22 = columns(j + 2, j), columns(j + 2, j + 1), columns(j + 2, j + 2)
            left.append(list(left2))
        left += [columns(i, j) for i in range(j + 3, count)]
        inside = (lane >= first) & (lane < first + TILE)
        lower = jnp.where(inside, (lane - first == sub).astype(F32), rows[j])
        both = lower
        scale = jnp.ones((TILE, LANES), F32)
        for i in range(TILE):
            inverse_pivot = 1.0 / row_of(here[i], i)
            by_others = here[i] * (inverse_pivot * others[i])
            by_below = here[i] * (inverse_pivot * below[i])
            if one:
                by_left1 = left1[i] * inverse_pivot
            if two:
                by_left2 = left2[i] * inverse_pivot
            for c in range(i + 1, TILE):
                pivot_row = row_of(here[c], i)
                here[c] = here[c] - by_others * pivot_row
                if one:
                    left1[c] = left1[c] - by_left1 * pivot_row
                if two:
                    left2[c] = left2[c] - by_left2 * pivot_row
            for c in range(TILE):
                if one:
                    pivot_row = row_of(left1[i], c)
                    ahead11[c] = ahead11[c] - by_left1 * pivot_row
                if two:
                    ahead21[c] = ahead21[c] - by_left2 * pivot_row
                    ahead22[c] = ahead22[c] - by_left2 * row_of(left2[i], c)
            lower = lower - by_below * row_of(lower, i)
            both = both - by_others * row_of(both, i)
            scale = jnp.where(sub == i, inverse_pivot, scale)
        rows[j] = lower * lax.rsqrt(1.0 / scale)
        if not one:
            break
        both = both * scale
        spread = [row_of(both, c) for c in range(TILE)]
        for i in range(j + 1, count):
            terms = [left[i - j - 1][c] * spread[c] for c in range(TILE)]
            while len(terms) > 1:
                terms = [terms[t] + terms[t + 1] for t in range(0, len(terms), 2)]
            rows[i] = jnp.where(inside, 0.0, rows[i]) - terms[0]
        here = ahead11
        if two:
            left1, ahead11 = ahead21, ahead22
    return rows


def dot6(a, b, dims):
    a1, a2, a3 = split3(a)
    b1, b2, b3 = split3(b)
    left, right = dims
    return lax.dot_general(
        jnp.concatenate([a1, a2, a1, a2, a1, a3], axis=left),
        jnp.concatenate([b1, b1, b2, b2, b3, b1], axis=right),
        (((left,), (right,)), ((), ())),
        preferred_element_type=F32,
    )


def dot6_twice(a, b):
    a1, a2, a3 = split3(a)
    b1, b2, b3 = split3(b)
    low = lax.broadcasted_iota(jnp.int32, a.shape, 1) < CORE
    first = jnp.where(low, a1.astype(F32), a2.astype(F32)).astype(BF16)
    second = jnp.where(low, a1.astype(F32), a3.astype(F32)).astype(BF16)
    return lax.dot_general(
        jnp.concatenate([first, first, second], axis=1),
        jnp.concatenate([b1, b1, b2, b2, b3, b1], axis=0),
        (((1,), (0,)), ((), ())),
        preferred_element_type=F32,
    )


def factor_in_place(matrix, finished):
    order = matrix.shape[0]
    for start in range(0, order, CORE):
        base = start // LANES * LANES
        half = start - base
        stop = start + CORE
        group = slice(base, base + LANES)
        block = matrix[start:stop, group]
        core = jnp.concatenate(
            inverse_factor([block[t : t + TILE] for t in range(0, CORE, TILE)], half), axis=0
        )
        sub = lax.broadcasted_iota(jnp.int32, (CORE, LANES), 0) + half
        lane = lax.broadcasted_iota(jnp.int32, (CORE, LANES), 1)
        inside = (lane >= half) & (lane < half + CORE)
        core = jnp.where(inside & (lane > sub), 0.0, core)
        placed = jnp.where(inside, core, 0.0)
        twice = jnp.concatenate([placed, placed], axis=0)
        matrix[start:stop, group] = core
        cuts = [(stop, stop + CORE), (stop + CORE, order)]
        cuts = [cut for cut in cuts if cut[0] < cut[1] <= order]
        factors = []
        for low, high in cuts:
            rows = matrix[low:high, group]
            factors.append(dot6(rows, twice, (1, 1)))
            lane = lax.broadcasted_iota(jnp.int32, (high - low, LANES), 1)
            inside = (lane >= half) & (lane < half + CORE)
            matrix[low:high, group] = jnp.where(inside, 0.0, rows)
        spans = [at for at in range(0, order, LANES) if at != base]
        spans = [at for at in spans if at > base] + [at for at in spans if at < base]
        solved = {base: core}
        for at in spans:
            both = matrix[base : base + LANES, at : at + LANES]
            solved[at] = dot6(placed, both, (1, 0))
        for at in spans:
            matrix[start:stop, at : at + LANES] = solved[at]
        for (low, high), factor in zip(cuts, factors):
            for at in [base] + spans:
                matrix[low:high, at : at + LANES] = matrix[low:high, at : at + LANES] - dot6_twice(
                    factor, solved[at]
                )
        if half:
            finished(base // LANES)


def update_kernel(
    panel_ref, got_ref, trailing_ref, panel_out, trailing_out,
    held_ref, solved_ref, matrix_ref, cov_ref, far_cov_ref, weight_ref, pieces_ref,
    even_high_ref, even_low_ref, odd_high_ref, odd_low_ref, own_ref, turned_ref, in_sem, panel_sem, out_sems,
):
    here_row = lax.axis_index("row")
    here_col = lax.axis_index("col")
    block_k = panel_ref[0]
    share = solved_ref.shape[2]
    span = held_ref.shape[2]
    fetch = pltpu.make_async_copy(trailing_ref, held_ref.at[pl.ds(0, LB)], in_sem)
    fetch.start()

    source = got_ref[block_k // LB, 2 * PER : 4 * PER, :]
    pivot_x = [source[t : t + 1] for t in range(PER)]
    pivot_y = [source[PER + t : PER + t + 1] for t in range(PER)]
    turned = source.T
    sub = lax.broadcasted_iota(jnp.int32, (LANES, LANES), 0)
    lane = lax.broadcasted_iota(jnp.int32, (LANES, LANES), 1)
    part = lane % TILE
    for t in range(PER):
        rows = slice(t * LANES, (t + 1) * LANES)
        wide_x = jnp.broadcast_to(turned[:, t : t + 1], (LANES, LANES))
        wide_y = jnp.broadcast_to(turned[:, PER + t : PER + t + 1], (LANES, LANES))
        for u in range(PER):
            cov = matern(wide_x, wide_y, pivot_x[u], pivot_y[u])
            if t == u:
                cov = cov + jnp.where(sub == lane, NUGGET, 0.0)
            matrix_ref[rows, u * LANES : (u + 1) * LANES] = cov
        x = (wide_x - 0.5) * SCALE
        y = (wide_y - 0.5) * SCALE
        value = jnp.where(part == 0, -2.0 * x, jnp.where(part == 1, -2.0 * y, 0.0))
        value = jnp.where(part == 2, 1.0, jnp.where(part == 3, x * x + y * y, value))
        first, second, third = (piece.astype(F32) for piece in split3(value))
        which = lane // TILE
        kept = jnp.where(
            (which == 0) | (which == 1) | (which == 4) | (which == 6), first,
            jnp.where((which == 2) | (which == 3) | (which == 7), second, jnp.where(which == 5, third, 0.0)),
        )
        kept = jnp.where(which == 6, second, jnp.where(which == 7, third, kept))
        pieces_ref[rows, :] = kept.astype(BF16)

    far = got_ref[(block_k + 1 + here_col // (B // span)) // LB, 4 * PER : 6 * PER, :].T
    for u in range(PER):
        at = slice(u * LANES, (u + 1) * LANES)
        far_cov_ref[:, at] = matern(far[:span, 0:1], far[span:, 0:1], pivot_x[u], pivot_y[u])

    line = here_col * share // LANES
    for l in range(LB):
        own_ref[l : l + 1, :] = got_ref[l, pl.ds(line, 1), :]
        own_ref[LB + l : LB + l + 1, :] = got_ref[l, pl.ds(PER + line, 1), :]
    turned_ref[:, : 2 * LB] = own_ref[...].T
    own = turned_ref[pl.ds(here_col * share % LANES, share), :]
    sub = lax.broadcasted_iota(jnp.int32, (share, LANES), 0)
    lane = lax.broadcasted_iota(jnp.int32, (share, LANES), 1)
    for l in range(LB):
        same = l * LB + here_row == block_k
        for u in range(PER):
            cov = matern(own[:, l : l + 1], own[:, LB + l : LB + l + 1], pivot_x[u], pivot_y[u])
            match = (lane + u * LANES == sub + here_col * share) & same
            cov_ref[l * share : (l + 1) * share, u * LANES : (u + 1) * LANES] = cov + jnp.where(
                match, NUGGET, 0.0
            )

    def finished(t):
        at = slice(t * LANES, (t + 1) * LANES)
        width = (t + 1) * LANES
        sub = lax.broadcasted_iota(jnp.int32, (LANES, width), 0) + t * LANES
        lane = lax.broadcasted_iota(jnp.int32, (LANES, width), 1)
        inverse = jnp.where(sub >= lane, matrix_ref[at, :width], 0.0)
        solved = dot6(cov_ref[:, :width], inverse, (1, 1))
        for l in range(LB):
            wanted = l * LB + here_row >= block_k
            solved_ref[l, 0, :, at] = jnp.where(wanted, solved[l * share : (l + 1) * share], 0.0)
        far_factor = dot6(far_cov_ref[:, :width], inverse, (1, 1))
        weight = dot6(far_factor, inverse, (1, 0))
        if t:
            weight_ref[:, : width - LANES] = weight_ref[:, : width - LANES] + weight[:, : width - LANES]
        weight_ref[:, width - LANES : width] = weight[:, width - LANES :]

    factor_in_place(matrix_ref, finished)
    panel_copy = pltpu.make_async_copy(solved_ref, panel_out, panel_sem)
    panel_copy.start()
    fetch.wait()

    begin = jnp.where(block_k < here_row, 0, (block_k - here_row + LB) // LB)

    def send(l):
        return pltpu.make_async_copy(held_ref.at[l], trailing_out.at[l], out_sems.at[l])

    def pass_on(l, carry):
        send(l).start()
        return carry

    lax.fori_loop(0, begin, pass_on, 0)
    weight_high, weight_low = split2(weight_ref[...])
    weights = jnp.concatenate([weight_high, weight_low], axis=0)

    def stacked(l):
        place = got_ref[l, 0 : 2 * PER, :]
        sub = lax.broadcasted_iota(jnp.int32, (TILE, LANES), 0)
        value = []
        for t in range(PER):
            x = (row_of(place, t) - 0.5) * SCALE
            y = (row_of(place, PER + t) - 0.5) * SCALE
            row = jnp.where(sub == 0, x, jnp.where(sub == 1, y, jnp.where(sub == 3, 1.0, 0.0)))
            value.append(jnp.where(sub == 2, x * x + y * y, row))
        first, second, third = (piece.astype(F32) for piece in split3(jnp.concatenate(value, axis=1)))
        zero = jnp.zeros_like(first)
        stack = [first, second, first, second, third, first, third, second] + [zero] * 8
        return jnp.concatenate(stack, axis=0).astype(BF16)

    def covariances(stack, part, high_ref, low_ref):
        rows = slice(part * ROWS, (part + 1) * ROWS)
        square = jnp.dot(pieces_ref[rows, :], stack, preferred_element_type=F32)
        square = jnp.maximum(square, 1e-30)
        scaled = square * lax.rsqrt(square)
        cov = (1.0 + scaled) * jnp.exp(-scaled)
        high_ref[rows, :], low_ref[rows, :] = split2(cov)

    def apply(l, part, high_ref, low_ref):
        slot = jnp.where(l >= begin, l, LB)
        at = slice(part * COLS, (part + 1) * COLS)
        both = jnp.dot(weights, high_ref[:, at], preferred_element_type=F32)
        low = jnp.dot(weight_high, low_ref[:, at], preferred_element_type=F32)
        held_ref[slot, 0, :, at] = held_ref[slot, 0, :, at] - (both[:span] + (both[span:] + low))

    def work(l, make, use):
        stack = stacked(l)
        for part in range(max(B // ROWS, B // COLS)):
            if part < B // ROWS:
                covariances(stack, part, *make)
            if part < B // COLS:
                apply(l - 1, part, *use)

    def send_from(l):
        @pl.when(l >= begin)
        def _():
            send(l).start()

    even = (even_high_ref, even_low_ref)
    odd = (odd_high_ref, odd_low_ref)

    @pl.when(begin < LB)
    def _():
        def step(pair, carry):
            l = 2 * pair
            work(l, even, odd)
            work(l + 1, odd, even)
            send_from(l - 1)
            send_from(l)
            return carry

        lax.fori_loop(begin // 2, LB // 2, step, 0)
        for part in range(B // COLS):
            apply(LB - 1, part, *odd)
        send(LB - 1).start()

    def finish(l, carry):
        send(l).wait()
        return carry

    lax.fori_loop(0, LB, finish, 0)
    panel_copy.wait()


def update(panel_index, got, trailing, share):
    span = trailing.shape[2]
    return pl.pallas_call(
        update_kernel,
        out_shape=(
            jax.ShapeDtypeStruct((LB, 1, share, B), F32),
            jax.ShapeDtypeStruct(trailing.shape, F32),
        ),
        in_specs=[
            pl.BlockSpec(memory_space=pltpu.SMEM),
            pl.BlockSpec(memory_space=pltpu.VMEM),
            pl.BlockSpec(memory_space=pl.ANY),
        ],
        out_specs=(
            pl.BlockSpec(memory_space=pl.ANY),
            pl.BlockSpec(memory_space=pl.ANY),
        ),
        scratch_shapes=[
            pltpu.VMEM((LB + 1,) + trailing.shape[1:], F32),
            pltpu.VMEM((LB, 1, share, B), F32),
            pltpu.VMEM((B, B), F32),
            pltpu.VMEM((LB * share, B), F32),
            pltpu.VMEM((span, B), F32),
            pltpu.VMEM((span, B), F32),
            pltpu.VMEM((B, LANES), BF16),
            pltpu.VMEM((B, B), BF16),
            pltpu.VMEM((B, B), BF16),
            pltpu.VMEM((B, B), BF16),
            pltpu.VMEM((B, B), BF16),
            pltpu.VMEM((2 * LB, LANES), F32),
            pltpu.VMEM((LANES, LANES), F32),
            pltpu.SemaphoreType.DMA,
            pltpu.SemaphoreType.DMA,
            pltpu.SemaphoreType.DMA((LB,)),
        ],
        compiler_params=pltpu.CompilerParams(vmem_limit_bytes=60 * 1024 * 1024),
        name="update",
    )(panel_index, got, trailing)


def on_device(coords, order, panel_index, trailing):
    share = B // lax.axis_size("col")
    got = lax.all_to_all(locate(panel_index, order, coords), "row", 0, 0, tiled=True)
    return update(panel_index, got, trailing, share)


def solution(mesh):
    placed = (P(None, "row"), P(), P(), P(None, "row", "col", None))
    return jax.shard_map(
        on_device,
        mesh=mesh,
        in_specs=placed,
        out_specs=(P(None, "row", "col", None), P(None, "row", "col", None)),
        check_vma=False,
    )
```

```python
import functools
import math

import jax
import jax.numpy as jnp
from jax import lax
from jax.experimental import pallas as pl
from jax.experimental.pallas import tpu as pltpu
from jax.sharding import PartitionSpec as P

B = 512
LB = 16
OWNED = LB * B
LANES = 128
PER = B // LANES
SCALE = math.sqrt(3.0) / 0.05
ROOT_THREE = math.sqrt(3.0)
LENGTH = 0.05
NUGGET = 1.0
F32 = jnp.float32
BF16 = jnp.bfloat16


def matern(row_x, row_y, col_x, col_y):
    diff_x = row_x - col_x
    diff_y = row_y - col_y
    square = diff_x * diff_x + diff_y * diff_y
    scaled = (ROOT_THREE / LENGTH) * square * lax.rsqrt(jnp.maximum(square, 1e-30))
    return (1.0 + scaled) * jnp.exp(-scaled)


def split2(value):
    high = value.astype(BF16)
    return high, (value - high.astype(F32)).astype(BF16)


def split3(value):
    first = value.astype(BF16)
    rest = value - first.astype(F32)
    second = rest.astype(BF16)
    return first, second, (rest - second.astype(F32)).astype(BF16)


def locate_kernel(panel_ref, order_ref, coords_ref, out_ref, index_ref, pair_ref, table_ref, found_ref, sems):
    here = lax.axis_index("row")
    here_col = lax.axis_index("col")
    rows = OWNED // LANES
    order_copy = pltpu.make_async_copy(
        order_ref.at[pl.ds(here * rows, rows), :], index_ref, sems.at[0]
    )
    coords_copy = pltpu.make_async_copy(coords_ref, pair_ref, sems.at[1])
    order_copy.start()
    coords_copy.start()
    coords_copy.wait()
    for high in range(rows):
        at = slice(high * LANES, (high + 1) * LANES)
        table_ref[high : high + 1, :LANES] = pair_ref[0:1, at]
        table_ref[high : high + 1, LANES:] = pair_ref[1:2, at]
    pieces = jnp.concatenate(split3(table_ref[...]), axis=0)
    order_copy.wait()
    high_iota = lax.broadcasted_iota(jnp.int32, (rows, B), 0)
    low_iota = lax.broadcasted_iota(jnp.int32, (LANES, B), 0)
    for block in range(LB):
        index = jnp.concatenate(
            [index_ref[block * PER + t : block * PER + t + 1, :] for t in range(PER)], axis=1
        )
        index = index - here * OWNED
        high = (high_iota == (index >> 7)).astype(F32).astype(BF16)
        spread = lax.dot_general(
            pieces,
            jnp.concatenate([high, high, high], axis=0),
            (((0,), (0,)), ((), ())),
            preferred_element_type=F32,
        )
        chosen = low_iota == (index & (LANES - 1))
        for axis in range(2):
            part = spread[axis * LANES : (axis + 1) * LANES]
            value = jnp.sum(jnp.where(chosen, part, 0.0), axis=0, keepdims=True)
            for t in range(PER):
                found_ref[block, axis * PER + t : axis * PER + t + 1, :] = value[
                    :, t * LANES : (t + 1) * LANES
                ]
    pivot = found_ref[jnp.clip(panel_ref[0] - here * LB, 0, LB - 1)]
    ahead = 1 + here_col // (2 * PER)
    local = jnp.clip(panel_ref[0] + ahead - here * LB, 0, LB - 1)
    line = here_col // 2 % PER
    far_x = found_ref[local, pl.ds(line, 1), :]
    far_y = found_ref[local, pl.ds(PER + line, 1), :]
    low = lax.broadcasted_iota(jnp.int32, (1, LANES), 1) < LANES // 2
    even = jnp.where(low, far_x, pltpu.roll(far_y, LANES // 2, 1))
    odd = jnp.where(low, pltpu.roll(far_x, LANES // 2, 1), far_y)
    far = jnp.broadcast_to(jnp.where(here_col % 2 == 0, even, odd), (2 * PER, LANES))
    for block in range(LB):
        out_ref[block, 0 : 2 * PER, :] = found_ref[block]
        out_ref[block, 2 * PER : 4 * PER, :] = pivot
        out_ref[block, 4 * PER : 6 * PER, :] = far


def locate(panel_index, order, coords):
    return pl.pallas_call(
        locate_kernel,
        out_shape=jax.ShapeDtypeStruct((LB, 6 * PER, LANES), F32),
        in_specs=[
            pl.BlockSpec(memory_space=pltpu.SMEM),
            pl.BlockSpec(memory_space=pl.ANY),
            pl.BlockSpec(memory_space=pl.ANY),
        ],
        out_specs=pl.BlockSpec(memory_space=pltpu.VMEM),
        scratch_shapes=[
            pltpu.VMEM((OWNED // LANES, LANES), jnp.int32),
            pltpu.VMEM(coords.shape, F32),
            pltpu.VMEM((OWNED // LANES, 2 * LANES), F32),
            pltpu.VMEM((LB, 2 * PER, LANES), F32),
            pltpu.SemaphoreType.DMA((2,)),
        ],
        name="locate",
    )(panel_index, order.reshape(-1, LANES), coords)


TILE = 8
CORE = 64
ROWS = 128
COLS = 256


def column_of(value, at):
    return jnp.broadcast_to(value[:, at : at + 1], (TILE, LANES))


def row_of(value, at):
    return jnp.broadcast_to(value[at : at + 1, :], (TILE, LANES))


def inverse_factor(rows, offset, between):
    rows = list(rows)
    count = len(rows)
    sub = lax.broadcasted_iota(jnp.int32, (TILE, LANES), 0)
    lane = lax.broadcasted_iota(jnp.int32, (TILE, LANES), 1)
    others = [(sub != i).astype(F32) for i in range(TILE)]
    below = [(sub > i).astype(F32) for i in range(TILE)]

    def columns(row, panel):
        return [column_of(rows[row], offset + TILE * panel + c) for c in range(TILE)]

    here = columns(0, 0)
    for j in range(count):
        first = offset + TILE * j
        one = j + 1 < count
        left = [columns(i, j) for i in range(j + 1, count)]
        if one:
            left1 = list(left[0])
            ahead = columns(j + 1, j + 1)
        inside = (lane >= first) & (lane < first + TILE)
        lower = jnp.where(inside, (lane - first == sub).astype(F32), rows[j])
        both = lower
        scale = jnp.ones((TILE, LANES), F32)
        for i in range(TILE):
            inverse_pivot = 1.0 / row_of(here[i], i)
            by_others = here[i] * (inverse_pivot * others[i])
            by_below = here[i] * (inverse_pivot * below[i])
            if one:
                by_left = left1[i] * inverse_pivot
            for c in range(i + 1, TILE):
                pivot_row = row_of(here[c], i)
                here[c] = here[c] - by_others * pivot_row
                if one:
                    left1[c] = left1[c] - by_left * pivot_row
            if one:
                for c in range(TILE):
                    ahead[c] = ahead[c] - by_left * row_of(left1[i], c)
            lower = lower - by_below * row_of(lower, i)
            if one:
                both = both - by_others * row_of(both, i)
            scale = jnp.where(sub == i, inverse_pivot, scale)
        rows[j] = lower * lax.rsqrt(1.0 / scale)
        between(count - j)
        if not one:
            break
        both = both * scale
        spread = [row_of(both, c) for c in range(TILE)]
        for i in range(j + 1, count):
            terms = [left[i - j - 1][c] * spread[c] for c in range(TILE)]
            while len(terms) > 1:
                terms = [terms[t] + terms[t + 1] for t in range(0, len(terms), 2)]
            rows[i] = jnp.where(inside, 0.0, rows[i]) - terms[0]
        here = ahead
    return rows


def dot6(a, b, dims):
    a1, a2, a3 = split3(a)
    b1, b2, b3 = split3(b)
    left, right = dims
    return lax.dot_general(
        jnp.concatenate([a1, a2, a1, a2, a1, a3], axis=left),
        jnp.concatenate([b1, b1, b2, b2, b3, b1], axis=right),
        (((left,), (right,)), ((), ())),
        preferred_element_type=F32,
    )


def dot6_twice(a, b):
    a1, a2, a3 = split3(a)
    b1, b2, b3 = split3(b)
    low = lax.broadcasted_iota(jnp.int32, a.shape, 1) < CORE
    first = jnp.where(low, a1.astype(F32), a2.astype(F32)).astype(BF16)
    second = jnp.where(low, a1.astype(F32), a3.astype(F32)).astype(BF16)
    return lax.dot_general(
        jnp.concatenate([first, first, second], axis=1),
        jnp.concatenate([b1, b1, b2, b2, b3, b1], axis=0),
        (((1,), (0,)), ((), ())),
        preferred_element_type=F32,
    )


def run_share(jobs, slots):
    for _ in range(-(-len(jobs) // slots)):
        jobs.pop(0)()


def factor_in_place(matrix, jobs, finished):
    order = matrix.shape[0]
    due = []

    def between(slots):
        run_share(due, slots)
        run_share(jobs, slots)

    for start in range(0, order, CORE):
        base = start // LANES * LANES
        half = start - base
        stop = start + CORE
        group = slice(base, base + LANES)
        block = matrix[start:stop, group]
        core = jnp.concatenate(
            inverse_factor([block[t : t + TILE] for t in range(0, CORE, TILE)], half, between), axis=0
        )
        sub = lax.broadcasted_iota(jnp.int32, (CORE, LANES), 0) + half
        lane = lax.broadcasted_iota(jnp.int32, (CORE, LANES), 1)
        inside = (lane >= half) & (lane < half + CORE)
        core = jnp.where(inside & (lane > sub), 0.0, core)
        placed = jnp.where(inside, core, 0.0)
        twice = jnp.concatenate([placed, placed], axis=0)
        matrix[start:stop, group] = core
        spans = [at for at in range(0, order, LANES) if at != base]
        spans = [at for at in spans if at > base] + [at for at in spans if at < base]
        solved = {base: core}
        factors = {}

        def solve(at, start=start, base=base, placed=placed, solved=solved):
            both = matrix[base : base + LANES, at : at + LANES]
            solved[at] = dot6(placed, both, (1, 0))
            matrix[start : start + CORE, at : at + LANES] = solved[at]

        def eliminate(low, high, half=half, group=group, twice=twice, factors=factors):
            rows = matrix[low:high, group]
            factors[low] = dot6(rows, twice, (1, 1))
            lane = lax.broadcasted_iota(jnp.int32, (high - low, LANES), 1)
            inside = (lane >= half) & (lane < half + CORE)
            matrix[low:high, group] = jnp.where(inside, 0.0, rows)

        def reduce(low, high, at, factors=factors, solved=solved):
            matrix[low:high, at : at + LANES] = matrix[low:high, at : at + LANES] - dot6_twice(
                factors[low], solved[at]
            )

        if stop < order:
            eliminate(stop, stop + CORE)
            ahead = base if not half else base + LANES
            if half:
                solve(ahead)
            reduce(stop, stop + CORE, ahead)
            rest = [at for at in spans if at not in solved]
            due += [functools.partial(solve, at) for at in rest]
            due += [functools.partial(reduce, stop, stop + CORE, at) for at in [base] + spans if at != ahead]
            if stop + CORE < order:
                due.append(functools.partial(eliminate, stop + CORE, order))
                due += [functools.partial(reduce, stop + CORE, order, at) for at in [base] + spans]
        else:
            for at in spans:
                solve(at)
        if half:
            jobs += finished(base // LANES)
    while jobs:
        jobs.pop(0)()


def update_kernel(
    panel_ref, got_ref, trailing_ref, panel_out, trailing_out,
    held_ref, solved_ref, matrix_ref, cov_ref, far_cov_ref, weight_ref, pieces_ref, stack_ref,
    even_high_ref, even_low_ref, odd_high_ref, odd_low_ref, own_ref, turned_ref, in_sem, panel_sem, out_sems,
):
    here_row = lax.axis_index("row")
    here_col = lax.axis_index("col")
    block_k = panel_ref[0]
    share = solved_ref.shape[2]
    span = held_ref.shape[2]
    fetch = pltpu.make_async_copy(trailing_ref, held_ref.at[pl.ds(0, LB)], in_sem)
    fetch.start()

    source = got_ref[block_k // LB, 2 * PER : 4 * PER, :]
    pivot_x = [source[t : t + 1] for t in range(PER)]
    pivot_y = [source[PER + t : PER + t + 1] for t in range(PER)]
    turned = source.T
    sub = lax.broadcasted_iota(jnp.int32, (LANES, LANES), 0)
    lane = lax.broadcasted_iota(jnp.int32, (LANES, LANES), 1)
    for t in range(PER):
        rows = slice(t * LANES, (t + 1) * LANES)
        wide_x = jnp.broadcast_to(turned[:, t : t + 1], (LANES, LANES))
        wide_y = jnp.broadcast_to(turned[:, PER + t : PER + t + 1], (LANES, LANES))
        for u in range(PER):
            cov = matern(wide_x, wide_y, pivot_x[u], pivot_y[u])
            if t == u:
                cov = cov + jnp.where(sub == lane, NUGGET, 0.0)
            matrix_ref[rows, u * LANES : (u + 1) * LANES] = cov

    def distance_rows(t):
        rows = slice(t * LANES, (t + 1) * LANES)
        lane = lax.broadcasted_iota(jnp.int32, (LANES, LANES), 1)
        part = lane % TILE
        x = (jnp.broadcast_to(turned[:, t : t + 1], (LANES, LANES)) - 0.5) * SCALE
        y = (jnp.broadcast_to(turned[:, PER + t : PER + t + 1], (LANES, LANES)) - 0.5) * SCALE
        value = jnp.where(part == 0, -2.0 * x, jnp.where(part == 1, -2.0 * y, 0.0))
        value = jnp.where(part == 2, 1.0, jnp.where(part == 3, x * x + y * y, value))
        first, second, third = (piece.astype(F32) for piece in split3(value))
        which = lane // TILE
        kept = jnp.where((which == 0) | (which == 1) | (which == 4), first, 0.0)
        kept = jnp.where((which == 2) | (which == 3) | (which == 6), second, kept)
        kept = jnp.where((which == 5) | (which == 7), third, kept)
        pieces_ref[rows, :] = kept.astype(BF16)

    def far_rows():
        far = got_ref[(block_k + 1 + here_col // (B // span)) // LB, 4 * PER : 6 * PER, :].T
        for u in range(PER):
            at = slice(u * LANES, (u + 1) * LANES)
            far_cov_ref[:, at] = matern(far[:span, 0:1], far[span:, 0:1], pivot_x[u], pivot_y[u])

    line = here_col * share // LANES
    for l in range(LB):
        own_ref[l : l + 1, :] = got_ref[l, pl.ds(line, 1), :]
        own_ref[LB + l : LB + l + 1, :] = got_ref[l, pl.ds(PER + line, 1), :]
    turned_ref[:, : 2 * LB] = own_ref[...].T
    own = turned_ref[pl.ds(here_col * share % LANES, share), :]

    def own_rows(l):
        sub = lax.broadcasted_iota(jnp.int32, (share, LANES), 0)
        lane = lax.broadcasted_iota(jnp.int32, (share, LANES), 1)
        same = l * LB + here_row == block_k
        rows = slice(l * share, (l + 1) * share)
        for u in range(PER):
            at = slice(u * LANES, (u + 1) * LANES)
            cov = matern(own[:, l : l + 1], own[:, LB + l : LB + l + 1], pivot_x[u], pivot_y[u])
            match = (lane + u * LANES == sub + here_col * share) & same
            cov = cov + jnp.where(match, NUGGET, 0.0)
            for piece, value in enumerate(split3(cov)):
                cov_ref[piece, rows, at] = value

    jobs = []
    for l in range(LB):
        jobs.append(functools.partial(own_rows, l))
    jobs.append(far_rows)
    for t in range(PER):
        jobs.append(functools.partial(distance_rows, t))

    def finished(t):
        at = slice(t * LANES, (t + 1) * LANES)
        width = (t + 1) * LANES
        inverse = []

        def far_part():
            sub = lax.broadcasted_iota(jnp.int32, (LANES, width), 0) + t * LANES
            lane = lax.broadcasted_iota(jnp.int32, (LANES, width), 1)
            inverse.append(jnp.where(sub >= lane, matrix_ref[at, :width], 0.0))
            b1, b2, b3 = split3(inverse[0])
            for place, piece in enumerate([b1, b1, b2, b2, b3, b1]):
                stack_ref[t % 2, :, place * width : (place + 1) * width] = piece
            far_factor = dot6(far_cov_ref[:, :width], inverse[0], (1, 1))
            inverse.append(far_factor)

        def weight_part():
            weight = dot6(inverse[1], inverse[0], (1, 0))
            if t:
                weight_ref[:, : width - LANES] = weight_ref[:, : width - LANES] + weight[:, : width - LANES]
            weight_ref[:, width - LANES : width] = weight[:, width - LANES :]

        def panel_part(quarter):
            count = LB // PER
            rows = slice(quarter * count * share, (quarter + 1) * count * share)
            a1, a2, a3 = (cov_ref[piece, rows, :width] for piece in range(3))
            solved = lax.dot_general(
                jnp.concatenate([a1, a2, a1, a2, a1, a3], axis=1),
                stack_ref[t % 2, :, : 6 * width],
                (((1,), (1,)), ((), ())),
                preferred_element_type=F32,
            )
            for i in range(count):
                l = quarter * count + i
                wanted = l * LB + here_row >= block_k
                solved_ref[l, 0, :, at] = jnp.where(wanted, solved[i * share : (i + 1) * share], 0.0)

        return [far_part] + [functools.partial(panel_part, q) for q in range(PER)] + [weight_part]

    factor_in_place(matrix_ref, jobs, finished)
    panel_copy = pltpu.make_async_copy(solved_ref, panel_out, panel_sem)
    panel_copy.start()
    fetch.wait()

    begin = jnp.where(block_k < here_row, 0, (block_k - here_row + LB) // LB)

    def send(l):
        return pltpu.make_async_copy(held_ref.at[l], trailing_out.at[l], out_sems.at[l])

    def pass_on(l, carry):
        send(l).start()
        return carry

    lax.fori_loop(0, begin, pass_on, 0)
    weight_high, weight_low = split2(weight_ref[...])
    weights = jnp.concatenate([weight_high, weight_low], axis=0)

    def stacked(l):
        place = got_ref[l, 0 : 2 * PER, :]
        sub = lax.broadcasted_iota(jnp.int32, (TILE, LANES), 0)
        value = []
        for t in range(PER):
            x = (row_of(place, t) - 0.5) * SCALE
            y = (row_of(place, PER + t) - 0.5) * SCALE
            row = jnp.where(sub == 0, x, jnp.where(sub == 1, y, jnp.where(sub == 3, 1.0, 0.0)))
            value.append(jnp.where(sub == 2, x * x + y * y, row))
        first, second, third = (piece.astype(F32) for piece in split3(jnp.concatenate(value, axis=1)))
        zero = jnp.zeros_like(first)
        stack = [first, second, first, second, third, first, third, second] + [zero] * 8
        return jnp.concatenate(stack, axis=0).astype(BF16)

    def covariances(stack, part, high_ref, low_ref):
        rows = slice(part * ROWS, (part + 1) * ROWS)
        square = jnp.dot(pieces_ref[rows, :], stack, preferred_element_type=F32)
        square = jnp.maximum(square, 1e-30)
        scaled = square * lax.rsqrt(square)
        cov = (1.0 + scaled) * jnp.exp(-scaled)
        high_ref[rows, :], low_ref[rows, :] = split2(cov)

    def apply(l, part, high_ref, low_ref):
        slot = jnp.where(l >= begin, l, LB)
        at = slice(part * COLS, (part + 1) * COLS)
        both = jnp.dot(weights, high_ref[:, at], preferred_element_type=F32)
        low = jnp.dot(weight_high, low_ref[:, at], preferred_element_type=F32)
        held_ref[slot, 0, :, at] = held_ref[slot, 0, :, at] - (both[:span] + (both[span:] + low))

    def work(l, make, use):
        stack = stacked(l)
        for part in range(max(B // ROWS, B // COLS)):
            if part < B // ROWS:
                covariances(stack, part, *make)
            if part < B // COLS:
                apply(l - 1, part, *use)

    def send_from(l):
        @pl.when(l >= begin)
        def _():
            send(l).start()

    even = (even_high_ref, even_low_ref)
    odd = (odd_high_ref, odd_low_ref)

    @pl.when(begin < LB)
    def _():
        def step(pair, carry):
            l = 2 * pair
            work(l, even, odd)
            work(l + 1, odd, even)
            send_from(l - 1)
            send_from(l)
            return carry

        lax.fori_loop(begin // 2, LB // 2, step, 0)
        for part in range(B // COLS):
            apply(LB - 1, part, *odd)
        send(LB - 1).start()

    def finish(l, carry):
        send(l).wait()
        return carry

    lax.fori_loop(0, LB, finish, 0)
    panel_copy.wait()


def update(panel_index, got, trailing, share):
    span = trailing.shape[2]
    return pl.pallas_call(
        update_kernel,
        out_shape=(
            jax.ShapeDtypeStruct((LB, 1, share, B), F32),
            jax.ShapeDtypeStruct(trailing.shape, F32),
        ),
        in_specs=[
            pl.BlockSpec(memory_space=pltpu.SMEM),
            pl.BlockSpec(memory_space=pltpu.VMEM),
            pl.BlockSpec(memory_space=pl.ANY),
        ],
        out_specs=(
            pl.BlockSpec(memory_space=pl.ANY),
            pl.BlockSpec(memory_space=pl.ANY),
        ),
        scratch_shapes=[
            pltpu.VMEM((LB + 1,) + trailing.shape[1:], F32),
            pltpu.VMEM((LB, 1, share, B), F32),
            pltpu.VMEM((B, B), F32),
            pltpu.VMEM((3, LB * share, B), BF16),
            pltpu.VMEM((span, B), F32),
            pltpu.VMEM((span, B), F32),
            pltpu.VMEM((B, LANES), BF16),
            pltpu.VMEM((2, LANES, 6 * B), BF16),
            pltpu.VMEM((B, B), BF16),
            pltpu.VMEM((B, B), BF16),
            pltpu.VMEM((B, B), BF16),
            pltpu.VMEM((B, B), BF16),
            pltpu.VMEM((2 * LB, LANES), F32),
            pltpu.VMEM((LANES, LANES), F32),
            pltpu.SemaphoreType.DMA,
            pltpu.SemaphoreType.DMA,
            pltpu.SemaphoreType.DMA((LB,)),
        ],
        compiler_params=pltpu.CompilerParams(vmem_limit_bytes=60 * 1024 * 1024),
        name="update",
    )(panel_index, got, trailing)


def on_device(coords, order, panel_index, trailing):
    share = B // lax.axis_size("col")
    got = lax.all_to_all(locate(panel_index, order, coords), "row", 0, 0, tiled=True)
    return update(panel_index, got, trailing, share)


def solution(mesh):
    placed = (P(None, "row"), P(), P(), P(None, "row", "col", None))
    return jax.shard_map(
        on_device,
        mesh=mesh,
        in_specs=placed,
        out_specs=(P(None, "row", "col", None), P(None, "row", "col", None)),
        check_vma=False,
    )
```

```python
import functools
import math

import jax
import jax.numpy as jnp
from jax import lax
from jax.experimental import pallas as pl
from jax.experimental.pallas import tpu as pltpu
from jax.sharding import PartitionSpec as P

B = 512
LB = 16
OWNED = LB * B
LANES = 128
PER = B // LANES
SCALE = math.sqrt(3.0) / 0.05
ROOT_THREE = math.sqrt(3.0)
LENGTH = 0.05
NUGGET = 1.0
F32 = jnp.float32
BF16 = jnp.bfloat16


def matern(row_x, row_y, col_x, col_y):
    diff_x = row_x - col_x
    diff_y = row_y - col_y
    square = diff_x * diff_x + diff_y * diff_y
    scaled = (ROOT_THREE / LENGTH) * square * lax.rsqrt(jnp.maximum(square, 1e-30))
    return (1.0 + scaled) * jnp.exp(-scaled)


def split2(value):
    high = value.astype(BF16)
    return high, (value - high.astype(F32)).astype(BF16)


def split3(value):
    first = value.astype(BF16)
    rest = value - first.astype(F32)
    second = rest.astype(BF16)
    return first, second, (rest - second.astype(F32)).astype(BF16)


def locate_kernel(panel_ref, order_ref, coords_ref, out_ref, index_ref, pair_ref, table_ref, found_ref, sems):
    here = lax.axis_index("row")
    here_col = lax.axis_index("col")
    rows = OWNED // LANES
    order_copy = pltpu.make_async_copy(
        order_ref.at[pl.ds(here * rows, rows), :], index_ref, sems.at[0]
    )
    coords_copy = pltpu.make_async_copy(coords_ref, pair_ref, sems.at[1])
    order_copy.start()
    coords_copy.start()
    coords_copy.wait()
    for high in range(rows):
        at = slice(high * LANES, (high + 1) * LANES)
        table_ref[high : high + 1, :LANES] = pair_ref[0:1, at]
        table_ref[high : high + 1, LANES:] = pair_ref[1:2, at]
    pieces = jnp.concatenate(split3(table_ref[...]), axis=0)
    order_copy.wait()
    high_iota = lax.broadcasted_iota(jnp.int32, (rows, B), 0)
    low_iota = lax.broadcasted_iota(jnp.int32, (LANES, B), 0)
    for block in range(LB):
        index = jnp.concatenate(
            [index_ref[block * PER + t : block * PER + t + 1, :] for t in range(PER)], axis=1
        )
        index = index - here * OWNED
        high = (high_iota == (index >> 7)).astype(F32).astype(BF16)
        spread = lax.dot_general(
            pieces,
            jnp.concatenate([high, high, high], axis=0),
            (((0,), (0,)), ((), ())),
            preferred_element_type=F32,
        )
        chosen = low_iota == (index & (LANES - 1))
        for axis in range(2):
            part = spread[axis * LANES : (axis + 1) * LANES]
            value = jnp.sum(jnp.where(chosen, part, 0.0), axis=0, keepdims=True)
            for t in range(PER):
                found_ref[block, axis * PER + t : axis * PER + t + 1, :] = value[
                    :, t * LANES : (t + 1) * LANES
                ]
    pivot = found_ref[jnp.clip(panel_ref[0] - here * LB, 0, LB - 1)]
    ahead = 1 + here_col // (2 * PER)
    local = jnp.clip(panel_ref[0] + ahead - here * LB, 0, LB - 1)
    line = here_col // 2 % PER
    far_x = found_ref[local, pl.ds(line, 1), :]
    far_y = found_ref[local, pl.ds(PER + line, 1), :]
    low = lax.broadcasted_iota(jnp.int32, (1, LANES), 1) < LANES // 2
    even = jnp.where(low, far_x, pltpu.roll(far_y, LANES // 2, 1))
    odd = jnp.where(low, pltpu.roll(far_x, LANES // 2, 1), far_y)
    far = jnp.broadcast_to(jnp.where(here_col % 2 == 0, even, odd), (2 * PER, LANES))
    for block in range(LB):
        out_ref[block, 0 : 2 * PER, :] = found_ref[block]
        out_ref[block, 2 * PER : 4 * PER, :] = pivot
        out_ref[block, 4 * PER : 6 * PER, :] = far


def locate(panel_index, order, coords):
    return pl.pallas_call(
        locate_kernel,
        out_shape=jax.ShapeDtypeStruct((LB, 6 * PER, LANES), F32),
        in_specs=[
            pl.BlockSpec(memory_space=pltpu.SMEM),
            pl.BlockSpec(memory_space=pl.ANY),
            pl.BlockSpec(memory_space=pl.ANY),
        ],
        out_specs=pl.BlockSpec(memory_space=pltpu.VMEM),
        scratch_shapes=[
            pltpu.VMEM((OWNED // LANES, LANES), jnp.int32),
            pltpu.VMEM(coords.shape, F32),
            pltpu.VMEM((OWNED // LANES, 2 * LANES), F32),
            pltpu.VMEM((LB, 2 * PER, LANES), F32),
            pltpu.SemaphoreType.DMA((2,)),
        ],
        name="locate",
    )(panel_index, order.reshape(-1, LANES), coords)


TILE = 8
CORE = 64
ROWS = 256
COLS = 256


def column_of(value, at):
    return jnp.broadcast_to(value[:, at : at + 1], (TILE, LANES))


def row_of(value, at):
    return jnp.broadcast_to(value[at : at + 1, :], (TILE, LANES))


def inverse_factor(rows, offset, between):
    rows = list(rows)
    count = len(rows)
    sub = lax.broadcasted_iota(jnp.int32, (TILE, LANES), 0)
    lane = lax.broadcasted_iota(jnp.int32, (TILE, LANES), 1)
    others = [(sub != i).astype(F32) for i in range(TILE)]
    below = [(sub > i).astype(F32) for i in range(TILE)]

    def columns(row, panel):
        return [column_of(rows[row], offset + TILE * panel + c) for c in range(TILE)]

    here = columns(0, 0)
    for j in range(count):
        first = offset + TILE * j
        one = j + 1 < count
        left = [columns(i, j) for i in range(j + 1, count)]
        if one:
            left1 = list(left[0])
            ahead = columns(j + 1, j + 1)
        inside = (lane >= first) & (lane < first + TILE)
        lower = jnp.where(inside, (lane - first == sub).astype(F32), rows[j])
        both = lower
        scale = jnp.ones((TILE, LANES), F32)
        for i in range(TILE):
            inverse_pivot = 1.0 / row_of(here[i], i)
            by_others = here[i] * (inverse_pivot * others[i])
            by_below = here[i] * (inverse_pivot * below[i])
            if one:
                by_left = left1[i] * inverse_pivot
            for c in range(i + 1, TILE):
                pivot_row = row_of(here[c], i)
                here[c] = here[c] - by_others * pivot_row
                if one:
                    left1[c] = left1[c] - by_left * pivot_row
            if one:
                for c in range(TILE):
                    ahead[c] = ahead[c] - by_left * row_of(left1[i], c)
            lower = lower - by_below * row_of(lower, i)
            if one:
                both = both - by_others * row_of(both, i)
            scale = jnp.where(sub == i, inverse_pivot, scale)
        rows[j] = lower * lax.rsqrt(1.0 / scale)
        between(count - j)
        if not one:
            break
        both = both * scale
        spread = [row_of(both, c) for c in range(TILE)]
        for i in range(j + 1, count):
            terms = [left[i - j - 1][c] * spread[c] for c in range(TILE)]
            while len(terms) > 1:
                terms = [terms[t] + terms[t + 1] for t in range(0, len(terms), 2)]
            rows[i] = jnp.where(inside, 0.0, rows[i]) - terms[0]
        here = ahead
    return rows


def dot6(a, b, dims):
    a1, a2, a3 = split3(a)
    b1, b2, b3 = split3(b)
    left, right = dims
    return lax.dot_general(
        jnp.concatenate([a1, a2, a1, a2, a1, a3], axis=left),
        jnp.concatenate([b1, b1, b2, b2, b3, b1], axis=right),
        (((left,), (right,)), ((), ())),
        preferred_element_type=F32,
    )


def dot6_twice(a, b):
    a1, a2, a3 = split3(a)
    b1, b2, b3 = split3(b)
    low = lax.broadcasted_iota(jnp.int32, a.shape, 1) < CORE
    first = jnp.where(low, a1.astype(F32), a2.astype(F32)).astype(BF16)
    second = jnp.where(low, a1.astype(F32), a3.astype(F32)).astype(BF16)
    return lax.dot_general(
        jnp.concatenate([first, first, second], axis=1),
        jnp.concatenate([b1, b1, b2, b2, b3, b1], axis=0),
        (((1,), (0,)), ((), ())),
        preferred_element_type=F32,
    )


def run_share(jobs, slots):
    for _ in range(-(-len(jobs) // slots)):
        jobs.pop(0)()


def factor_in_place(matrix, jobs, finished):
    order = matrix.shape[0]
    due = []

    def between(slots):
        run_share(due, slots)
        run_share(jobs, slots)

    for start in range(0, order, CORE):
        base = start // LANES * LANES
        half = start - base
        stop = start + CORE
        group = slice(base, base + LANES)
        block = matrix[start:stop, group]
        core = jnp.concatenate(
            inverse_factor([block[t : t + TILE] for t in range(0, CORE, TILE)], half, between), axis=0
        )
        sub = lax.broadcasted_iota(jnp.int32, (CORE, LANES), 0) + half
        lane = lax.broadcasted_iota(jnp.int32, (CORE, LANES), 1)
        inside = (lane >= half) & (lane < half + CORE)
        core = jnp.where(inside & (lane > sub), 0.0, core)
        placed = jnp.where(inside, core, 0.0)
        twice = jnp.concatenate([placed, placed], axis=0)
        matrix[start:stop, group] = core
        spans = [at for at in range(0, order, LANES) if at != base]
        spans = [at for at in spans if at > base] + [at for at in spans if at < base]
        solved = {base: core}
        factors = {}

        def solve(at, start=start, base=base, placed=placed, solved=solved):
            both = matrix[base : base + LANES, at : at + LANES]
            solved[at] = dot6(placed, both, (1, 0))
            matrix[start : start + CORE, at : at + LANES] = solved[at]

        def eliminate(low, high, half=half, group=group, twice=twice, factors=factors):
            rows = matrix[low:high, group]
            factors[low] = dot6(rows, twice, (1, 1))
            lane = lax.broadcasted_iota(jnp.int32, (high - low, LANES), 1)
            inside = (lane >= half) & (lane < half + CORE)
            matrix[low:high, group] = jnp.where(inside, 0.0, rows)

        def reduce(low, high, at, factors=factors, solved=solved):
            matrix[low:high, at : at + LANES] = matrix[low:high, at : at + LANES] - dot6_twice(
                factors[low], solved[at]
            )

        if stop < order:
            eliminate(stop, stop + CORE)
            ahead = base if not half else base + LANES
            if half:
                solve(ahead)
            reduce(stop, stop + CORE, ahead)
            rest = [at for at in spans if at not in solved]
            due += [functools.partial(solve, at) for at in rest]
            due += [functools.partial(reduce, stop, stop + CORE, at) for at in [base] + spans if at != ahead]
            if stop + CORE < order:
                due.append(functools.partial(eliminate, stop + CORE, order))
                due += [functools.partial(reduce, stop + CORE, order, at) for at in [base] + spans]
        else:
            for at in spans:
                solve(at)
        if half:
            jobs += finished(base // LANES)
    while jobs:
        jobs.pop(0)()


def update_kernel(
    panel_ref, got_ref, trailing_ref, panel_out, trailing_out,
    held_ref, solved_ref, matrix_ref, cov_ref, far_cov_ref, weight_ref, pieces_ref, stack_ref,
    even_high_ref, even_low_ref, odd_high_ref, odd_low_ref, own_ref, turned_ref, in_sem, panel_sem, out_sems,
):
    here_row = lax.axis_index("row")
    here_col = lax.axis_index("col")
    block_k = panel_ref[0]
    share = solved_ref.shape[2]
    span = held_ref.shape[2]
    fetch = pltpu.make_async_copy(trailing_ref, held_ref.at[pl.ds(0, LB)], in_sem)
    fetch.start()

    source = got_ref[block_k // LB, 2 * PER : 4 * PER, :]
    pivot_x = [source[t : t + 1] for t in range(PER)]
    pivot_y = [source[PER + t : PER + t + 1] for t in range(PER)]
    turned = source.T
    sub = lax.broadcasted_iota(jnp.int32, (LANES, LANES), 0)
    lane = lax.broadcasted_iota(jnp.int32, (LANES, LANES), 1)
    for t in range(PER):
        rows = slice(t * LANES, (t + 1) * LANES)
        wide_x = jnp.broadcast_to(turned[:, t : t + 1], (LANES, LANES))
        wide_y = jnp.broadcast_to(turned[:, PER + t : PER + t + 1], (LANES, LANES))
        for u in range(PER):
            cov = matern(wide_x, wide_y, pivot_x[u], pivot_y[u])
            if t == u:
                cov = cov + jnp.where(sub == lane, NUGGET, 0.0)
            matrix_ref[rows, u * LANES : (u + 1) * LANES] = cov

    def distance_rows(t):
        rows = slice(t * LANES, (t + 1) * LANES)
        lane = lax.broadcasted_iota(jnp.int32, (LANES, LANES), 1)
        part = lane % TILE
        x = (jnp.broadcast_to(turned[:, t : t + 1], (LANES, LANES)) - 0.5) * SCALE
        y = (jnp.broadcast_to(turned[:, PER + t : PER + t + 1], (LANES, LANES)) - 0.5) * SCALE
        value = jnp.where(part == 0, -2.0 * x, jnp.where(part == 1, -2.0 * y, 0.0))
        value = jnp.where(part == 2, 1.0, jnp.where(part == 3, x * x + y * y, value))
        first, second, third = (piece.astype(F32) for piece in split3(value))
        which = lane // TILE
        kept = jnp.where((which == 0) | (which == 1) | (which == 4), first, 0.0)
        kept = jnp.where((which == 2) | (which == 3) | (which == 6), second, kept)
        kept = jnp.where((which == 5) | (which == 7), third, kept)
        pieces_ref[rows, :] = kept.astype(BF16)

    def far_rows():
        far = got_ref[(block_k + 1 + here_col // (B // span)) // LB, 4 * PER : 6 * PER, :].T
        for u in range(PER):
            at = slice(u * LANES, (u + 1) * LANES)
            far_cov_ref[:, at] = matern(far[:span, 0:1], far[span:, 0:1], pivot_x[u], pivot_y[u])

    line = here_col * share // LANES
    for l in range(LB):
        own_ref[l : l + 1, :] = got_ref[l, pl.ds(line, 1), :]
        own_ref[LB + l : LB + l + 1, :] = got_ref[l, pl.ds(PER + line, 1), :]
    turned_ref[:, : 2 * LB] = own_ref[...].T
    own = turned_ref[pl.ds(here_col * share % LANES, share), :]

    def own_rows(l):
        sub = lax.broadcasted_iota(jnp.int32, (share, LANES), 0)
        lane = lax.broadcasted_iota(jnp.int32, (share, LANES), 1)
        same = l * LB + here_row == block_k
        rows = slice(l * share, (l + 1) * share)
        for u in range(PER):
            at = slice(u * LANES, (u + 1) * LANES)
            cov = matern(own[:, l : l + 1], own[:, LB + l : LB + l + 1], pivot_x[u], pivot_y[u])
            match = (lane + u * LANES == sub + here_col * share) & same
            cov = cov + jnp.where(match, NUGGET, 0.0)
            for piece, value in enumerate(split3(cov)):
                cov_ref[piece, rows, at] = value

    jobs = []
    for l in range(LB):
        jobs.append(functools.partial(own_rows, l))
    jobs.append(far_rows)
    for t in range(PER):
        jobs.append(functools.partial(distance_rows, t))

    def finished(t):
        at = slice(t * LANES, (t + 1) * LANES)
        width = (t + 1) * LANES
        inverse = []

        def far_part():
            sub = lax.broadcasted_iota(jnp.int32, (LANES, width), 0) + t * LANES
            lane = lax.broadcasted_iota(jnp.int32, (LANES, width), 1)
            inverse.append(jnp.where(sub >= lane, matrix_ref[at, :width], 0.0))
            b1, b2, b3 = split3(inverse[0])
            for place, piece in enumerate([b1, b1, b2, b2, b3, b1]):
                stack_ref[t % 2, :, place * width : (place + 1) * width] = piece
            far_factor = dot6(far_cov_ref[:, :width], inverse[0], (1, 1))
            inverse.append(far_factor)

        def weight_part():
            weight = dot6(inverse[1], inverse[0], (1, 0))
            if t:
                weight_ref[:, : width - LANES] = weight_ref[:, : width - LANES] + weight[:, : width - LANES]
            weight_ref[:, width - LANES : width] = weight[:, width - LANES :]

        def panel_part(quarter):
            count = LB // PER
            rows = slice(quarter * count * share, (quarter + 1) * count * share)
            a1, a2, a3 = (cov_ref[piece, rows, :width] for piece in range(3))
            solved = lax.dot_general(
                jnp.concatenate([a1, a2, a1, a2, a1, a3], axis=1),
                stack_ref[t % 2, :, : 6 * width],
                (((1,), (1,)), ((), ())),
                preferred_element_type=F32,
            )
            for i in range(count):
                l = quarter * count + i
                wanted = l * LB + here_row >= block_k
                solved_ref[l, 0, :, at] = jnp.where(wanted, solved[i * share : (i + 1) * share], 0.0)

        return [far_part] + [functools.partial(panel_part, q) for q in range(PER)] + [weight_part]

    factor_in_place(matrix_ref, jobs, finished)
    panel_copy = pltpu.make_async_copy(solved_ref, panel_out, panel_sem)
    panel_copy.start()
    fetch.wait()

    begin = jnp.where(block_k < here_row, 0, (block_k - here_row + LB) // LB)

    def send(l):
        return pltpu.make_async_copy(held_ref.at[l], trailing_out.at[l], out_sems.at[l])

    def pass_on(l, carry):
        send(l).start()
        return carry

    lax.fori_loop(0, begin, pass_on, 0)
    weight_high, weight_low = split2(weight_ref[...])
    weights = jnp.concatenate([weight_high, weight_low], axis=0)

    def stacked(l):
        place = got_ref[l, 0 : 2 * PER, :]
        sub = lax.broadcasted_iota(jnp.int32, (TILE, LANES), 0)
        value = []
        for t in range(PER):
            x = (row_of(place, t) - 0.5) * SCALE
            y = (row_of(place, PER + t) - 0.5) * SCALE
            row = jnp.where(sub == 0, x, jnp.where(sub == 1, y, jnp.where(sub == 3, 1.0, 0.0)))
            value.append(jnp.where(sub == 2, x * x + y * y, row))
        first, second, third = (piece.astype(F32) for piece in split3(jnp.concatenate(value, axis=1)))
        zero = jnp.zeros_like(first)
        stack = [first, second, first, second, third, first, third, second] + [zero] * 8
        return jnp.concatenate(stack, axis=0).astype(BF16)

    def covariances(stack, part, high_ref, low_ref):
        rows = slice(part * ROWS, (part + 1) * ROWS)
        square = jnp.dot(pieces_ref[rows, :], stack, preferred_element_type=F32)
        square = jnp.maximum(square, 1e-30)
        scaled = square * lax.rsqrt(square)
        cov = (1.0 + scaled) * jnp.exp2(scaled * -math.log2(math.e))
        high_ref[rows, :], low_ref[rows, :] = split2(cov)

    def apply(l, part, high_ref, low_ref):
        slot = jnp.where(l >= begin, l, LB)
        at = slice(part * COLS, (part + 1) * COLS)
        both = jnp.dot(weights, high_ref[:, at], preferred_element_type=F32)
        low = jnp.dot(weight_high, low_ref[:, at], preferred_element_type=F32)
        held_ref[slot, 0, :, at] = held_ref[slot, 0, :, at] - (both[:span] + (both[span:] + low))

    def work(l, make, use):
        stack = stacked(l)
        for part in range(max(B // ROWS, B // COLS)):
            if part < B // ROWS:
                covariances(stack, part, *make)
            if part < B // COLS:
                apply(l - 1, part, *use)

    def send_from(l):
        @pl.when(l >= begin)
        def _():
            send(l).start()

    even = (even_high_ref, even_low_ref)
    odd = (odd_high_ref, odd_low_ref)

    @pl.when(begin < LB)
    def _():
        def step(pair, carry):
            l = 2 * pair
            work(l, even, odd)
            work(l + 1, odd, even)
            send_from(l - 1)
            send_from(l)
            return carry

        lax.fori_loop(begin // 2, LB // 2, step, 0)
        for part in range(B // COLS):
            apply(LB - 1, part, *odd)
        send(LB - 1).start()

    def finish(l, carry):
        send(l).wait()
        return carry

    lax.fori_loop(0, LB, finish, 0)
    panel_copy.wait()


def update(panel_index, got, trailing, share):
    span = trailing.shape[2]
    return pl.pallas_call(
        update_kernel,
        out_shape=(
            jax.ShapeDtypeStruct((LB, 1, share, B), F32),
            jax.ShapeDtypeStruct(trailing.shape, F32),
        ),
        in_specs=[
            pl.BlockSpec(memory_space=pltpu.SMEM),
            pl.BlockSpec(memory_space=pltpu.VMEM),
            pl.BlockSpec(memory_space=pl.ANY),
        ],
        out_specs=(
            pl.BlockSpec(memory_space=pl.ANY),
            pl.BlockSpec(memory_space=pl.ANY),
        ),
        scratch_shapes=[
            pltpu.VMEM((LB + 1,) + trailing.shape[1:], F32),
            pltpu.VMEM((LB, 1, share, B), F32),
            pltpu.VMEM((B, B), F32),
            pltpu.VMEM((3, LB * share, B), BF16),
            pltpu.VMEM((span, B), F32),
            pltpu.VMEM((span, B), F32),
            pltpu.VMEM((B, LANES), BF16),
            pltpu.VMEM((2, LANES, 6 * B), BF16),
            pltpu.VMEM((B, B), BF16),
            pltpu.VMEM((B, B), BF16),
            pltpu.VMEM((B, B), BF16),
            pltpu.VMEM((B, B), BF16),
            pltpu.VMEM((2 * LB, LANES), F32),
            pltpu.VMEM((LANES, LANES), F32),
            pltpu.SemaphoreType.DMA,
            pltpu.SemaphoreType.DMA,
            pltpu.SemaphoreType.DMA((LB,)),
        ],
        compiler_params=pltpu.CompilerParams(vmem_limit_bytes=60 * 1024 * 1024),
        name="update",
    )(panel_index, got, trailing)


def on_device(coords, order, panel_index, trailing):
    share = B // lax.axis_size("col")
    got = lax.all_to_all(locate(panel_index, order, coords), "row", 0, 0, tiled=True)
    return update(panel_index, got, trailing, share)


def solution(mesh):
    placed = (P(None, "row"), P(), P(), P(None, "row", "col", None))
    return jax.shard_map(
        on_device,
        mesh=mesh,
        in_specs=placed,
        out_specs=(P(None, "row", "col", None), P(None, "row", "col", None)),
        check_vma=False,
    )
```
